32 devices in a mesh: dp: 8 (over y, x, core), mp: 4 (over z).
Axes of the slice: x: 2, y: 2, z: 4, core: 2. Of those that a mesh axis runs over, the one named last changes fastest.
Arguments:
- tokens: bfloat16 [8192, 6144], P('dp', 'mp'), may hold values from -6 to 6
- dest_pos: int32 [8192], P('dp'), may hold values from 0 to 8191, as said below
- src_row: int32 [8192], P('dp'), may hold values from 0 to 8191, as said below
- segment_ids: int32 [8192], P('dp'), may hold values from 0 to 7, as said below
- norm_gain: float32 [6144], replicated, may hold values from 0.1 to 1.9
- qkv_weight: bfloat16 [3, 6144, 3072], P(None, None, 'mp'), may hold values from -0.078125 to 0.078125
- qk_gain: float32 [2, 24, 128], P(None, 'mp'), may hold values from 0.5 to 12
- out_weight: bfloat16 [3072, 6144], P('mp'), may hold values from -0.109375 to 0.109375
Outputs:
- updated: bfloat16 [8192, 6144], P('dp', 'mp')
The draws below stay inside these ranges and needn't reach their ends.
Inputs may be any that keep to these rules, and one draw needn't show every extreme that they name: `dest_pos`: each index of dp holds 1024 image rows and sends one contiguous block of whole patch rows (16 rows each) to every sequence, the rows keeping their order there; the block sizes of one index of dp are the same numbers for every index, in another order, the largest exactly 192; every sequence receives one block of each size, in a drawn order; each position is named once. `src_row`: the inverse of dest_pos. `segment_ids`: the index of the received block that a position lies in, counted within its sequence; never falling along a sequence.
All inputs are finite; a program needn't handle non-finite values.
Results may differ from the reference program's by a relative error of at most 0.012.
The reference program's roundings to bfloat16 on the way (of `packed`, `normed`, `value`, `weights`, `context` and `packed_out`) count: a program that leaves them out, or rounds other values in their place, can miss the bound.
Values may be sent and summed in bfloat16 or wider, within the bound.
No kernel may reach another device: no remote copies, remote signals or barrier semaphores. Data moves between devices by JAX's collectives and lax.ppermute only.
A program may use at most 192 MiB of HBM per device.

```python
import math
import jax
import jax.numpy as jnp
from jax import lax

D = 6144
HEAD_DIM = 128
HEADS = 24
SEQ_LEN = 1024
ROW = 16
CAP = 192
TOKENS = 8192
N_DP = 8


def packing(key):
    count = N_DP
    units = SEQ_LEN // ROW
    cap_units = CAP // ROW
    remain = units - cap_units
    share = remain // (count - 1)
    surplus = remain % (count - 1)
    flows = jnp.arange(count, dtype=jnp.int32)
    sizes = jnp.where(flows == 0, cap_units, share + (flows - 1 < surplus).astype(jnp.int32)).astype(jnp.int32) * ROW
    subkeys = jax.random.split(jax.random.fold_in(key, 7), 4)
    sigma = jax.random.permutation(subkeys[0], count).astype(jnp.int32)
    tau = jax.random.permutation(subkeys[1], count).astype(jnp.int32)
    target = tau[(sigma[:, None] + flows[None, :]) % count]

    def starts(subkey):
        scores = jax.random.randint(subkey, (count, count), 0, 1 << 20, dtype=jnp.int32) * count + flows[None, :]
        order = jnp.argsort(scores, axis=1).astype(jnp.int32)
        ordered = sizes[order]
        begin = jnp.cumsum(ordered, axis=1) - ordered
        rank = jnp.argsort(order, axis=1).astype(jnp.int32)
        return jnp.take_along_axis(begin, rank, axis=1).astype(jnp.int32)
    src_start = starts(subkeys[2])
    dst_start = starts(subkeys[3])
    positions = jnp.arange(SEQ_LEN, dtype=jnp.int32)
    inside = (positions[None, :, None] >= src_start[:, None, :]) & (positions[None, :, None] < src_start[:, None, :] + sizes[None, None, :])
    flow_of = jnp.sum(inside.astype(jnp.int32) * flows[None, None, :], axis=2).astype(jnp.int32)
    offset = positions[None, :] - jnp.take_along_axis(src_start, flow_of, axis=1)
    dest_seq = jnp.take_along_axis(target, flow_of, axis=1)
    dest_begin = dst_start[dest_seq, flow_of]
    dest_pos = (dest_seq * SEQ_LEN + dest_begin + offset).reshape(-1).astype(jnp.int32)
    src_row = jnp.zeros((N_DP * SEQ_LEN,), jnp.int32).at[dest_pos].set(jnp.arange(N_DP * SEQ_LEN, dtype=jnp.int32))
    segment = jnp.sum((positions[None, :, None] >= dst_start[:, None, :]).astype(jnp.int32), axis=2) - 1
    return (dest_pos, src_row, segment.reshape(-1).astype(jnp.int32))


def draw_dest_pos(key, part):
    return packing(key)[0]


def draw_src_row(key, part):
    return packing(key)[1]


def draw_segment_ids(key, part):
    return packing(key)[2]


def draw_qk_gain(key, part):
    first, second = jax.random.split(jax.random.fold_in(key, 11))
    level_draw = jax.random.uniform(first, (2, HEADS, 1), jnp.float32, 0.0, 1.0)
    level = 1.2 * jnp.exp(level_draw * jnp.log(2.5))
    rough = jax.random.uniform(second, (2, HEADS, HEAD_DIM), jnp.float32, 0.8, 1.2)
    return (level * rough).astype(jnp.float32)


def steps_of(rng, dims, shards, smallest, high):
    def one(dim, shards_of):
        steps = jax.random.uniform(jax.random.fold_in(jax.random.fold_in(rng, 6), dim), (shards_of,), jnp.float32, smallest / len(shards), high / len(shards))
        return jnp.repeat(jnp.exp(steps), dims[dim] // shards_of).reshape((-1,) + (1,) * (len(dims) - dim - 1))

    level = one(*shards[0])
    for cut in shards[1:]:
        level = level * one(*cut)
    return level


def normal_values(own_key, extent, width, reach, cuts=(), held_as=jnp.bfloat16):
    array = jax.random.normal(own_key, extent, jnp.float32) * width
    if len(cuts) > 0:
        array = steps_of(own_key, extent, cuts, -0.22, 0.18) * array
    return jnp.clip(array, min=-reach, max=reach).astype(held_as)


def setup_inputs(seed: int = 0) -> dict:
    splits = jax.random.split(jax.random.key(seed), 9)
    tokens = normal_values(splits[0], (TOKENS, D), 1.0, 6.0, ((0, 8), (1, 4)))
    dest_pos = draw_dest_pos(jax.random.fold_in(splits[8], 71), 0)
    src_row = draw_src_row(jax.random.fold_in(splits[8], 71), 0)
    segment_ids = draw_segment_ids(jax.random.fold_in(splits[8], 71), 0)
    norm_gain = jnp.clip(1.0 + 0.18 * jax.random.normal(splits[4], (D,), jnp.float32), 0.1, 1.9)
    qkv_weight = normal_values(splits[5], (3, D, HEADS * HEAD_DIM), D ** -0.5, 0.078125, ((2, 4),))
    qk_gain = draw_qk_gain(jax.random.fold_in(splits[8], 71), 0)
    out_weight = normal_values(splits[7], (HEADS * HEAD_DIM, D), (HEADS * HEAD_DIM) ** -0.5, 0.109375, ((0, 4),))
    return {"tokens": tokens, "dest_pos": dest_pos, "src_row": src_row, "segment_ids": segment_ids, "norm_gain": norm_gain, "qkv_weight": qkv_weight, "qk_gain": qk_gain, "out_weight": out_weight}


EPS = 1e-06
NEG = -1e+30

def norm_rows(values, gain):
    average = lax.optimization_barrier(jnp.mean(values, axis=-1, keepdims=True))
    centred = values - average
    variance = lax.optimization_barrier(jnp.mean(centred * centred, axis=-1, keepdims=True))
    return centred * lax.rsqrt(variance + EPS) * gain

def sequence_layer(packed, segment, norm_gain, qkv_weight, qk_gain, out_weight):
    normed = norm_rows(packed.astype(jnp.float32), norm_gain).astype(jnp.bfloat16)
    shape = (SEQ_LEN, HEADS, HEAD_DIM)
    query = jnp.dot(normed, qkv_weight[0], preferred_element_type=jnp.float32).reshape(shape)
    key_part = jnp.dot(normed, qkv_weight[1], preferred_element_type=jnp.float32).reshape(shape)
    value = jnp.dot(normed, qkv_weight[2], preferred_element_type=jnp.float32).reshape(shape)
    query = norm_rows(query, qk_gain[0]).astype(jnp.bfloat16)
    key_norm = norm_rows(key_part, qk_gain[1]).astype(jnp.bfloat16)
    value = value.astype(jnp.bfloat16)
    scale = 1.0 / math.sqrt(HEAD_DIM)
    scores = jnp.einsum('qhd,khd->hqk', query.astype(jnp.float32), key_norm.astype(jnp.float32)) * scale
    allowed = segment[:, None] == segment[None, :]
    scores = jnp.where(allowed[None], scores, NEG)
    top = lax.optimization_barrier(jnp.max(scores, axis=-1, keepdims=True))
    expo = jnp.exp(scores - top)
    weights = (expo / lax.optimization_barrier(jnp.sum(expo, axis=-1, keepdims=True))).astype(jnp.bfloat16)
    context = jnp.einsum('hqk,khd->qhd', weights.astype(jnp.float32), value.astype(jnp.float32))
    context = context.astype(jnp.bfloat16).reshape(SEQ_LEN, HEADS * HEAD_DIM)
    branch = jnp.dot(context, out_weight, preferred_element_type=jnp.float32)
    return (packed.astype(jnp.float32) + branch).astype(jnp.bfloat16)

def reference(tokens, dest_pos, src_row, segment_ids, norm_gain, qkv_weight, qk_gain, out_weight):
    packed = tokens[src_row].reshape(N_DP, SEQ_LEN, D)
    segments = segment_ids.reshape(N_DP, SEQ_LEN)

    def one_sequence(item):
        return sequence_layer(item[0], item[1], norm_gain, qkv_weight, qk_gain, out_weight)
    packed_out = lax.map(one_sequence, (packed, segments))
    return packed_out.reshape(N_DP * SEQ_LEN, D)[dest_pos]
```

```python
import functools
import math

import jax
import jax.numpy as jnp
import numpy as np
from jax import lax
from jax.experimental import pallas as pl
from jax.experimental.pallas import tpu as pltpu
from jax.sharding import PartitionSpec as P

HEAD_DIM = 128
EPS = 1e-06
NEG = -1e30
VMEM = 56 * 1024 * 1024


def pick(total, wanted):
    return max(w for w in range(128, min(total, wanted) + 1, 128) if total % w == 0)


def line_schedule(n):
    steps = {}
    for s in range(1, n):
        for kind, low in (("E", 0), ("O", 1)):
            pairs = []
            for i in range(low, n - 1, 2):
                if i - s + 1 >= 0:
                    pairs.append((i, i + 1))
                if i + s <= n - 1:
                    pairs.append((i + 1, i))
            if pairs:
                steps[(s, kind)] = pairs
    slots = [[] for _ in range(n)]
    for (s, kind), pairs in sorted(steps.items()):
        for source, target in pairs:
            origin = target - s if source < target else target + s
            slots[target].append(((s, kind), origin))
    return steps, slots


def relay(block, axis, n):
    steps, slots = line_schedule(n)
    got = {}
    for s, kind in sorted(steps):
        other = "O" if kind == "E" else "E"
        source = block if s == 1 else got[(s - 1, other)]
        got[(s, kind)] = lax.ppermute(source, axis, steps[(s, kind)])
    place = lax.axis_index(axis)
    arrived = []
    for k in range(n - 1):
        keys = sorted({slots[i][k][0] for i in range(n)})
        value = got[keys[0]]
        for key in keys[1:]:
            here = np.array([slots[i][k][0] == key for i in range(n)])
            value = jnp.where(jnp.asarray(here)[place], got[key], value)
        arrived.append(value)
    return arrived


def origins(axis, n):
    _, slots = line_schedule(n)
    table = np.array([[slots[i][k][1] for k in range(n - 1)] for i in range(n)], np.int32)
    place = lax.axis_index(axis)
    return [jnp.asarray(table)[place, k] for k in range(n - 1)]


def project(x, weight, which, acc):
    rows, depth = x.shape
    kinds, _, width = weight.shape
    cols = pick(width, 384)

    def kernel(which_ref, x_ref, w_ref, *refs):
        part = jnp.dot(x_ref[...], w_ref[...], preferred_element_type=jnp.float32)
        if len(refs) == 2:
            part = part + refs[0][...]
        refs[-1][...] = part

    tile = pl.BlockSpec((None, rows, cols), lambda c, j, w: (c, 0, j))
    in_specs = [
        pl.BlockSpec((rows, depth), lambda c, j, w: (0, 0)),
        pl.BlockSpec((None, depth, cols), lambda c, j, w: (c, w[0], j)),
    ]
    args = [jnp.reshape(which, (1,)), x, weight]
    aliases = {}
    if acc is not None:
        in_specs.append(tile)
        args.append(acc)
        aliases = {3: 0}
    return pl.pallas_call(
        kernel,
        grid_spec=pltpu.PrefetchScalarGridSpec(
            num_scalar_prefetch=1,
            grid=(kinds, width // cols),
            in_specs=in_specs,
            out_specs=tile,
        ),
        out_shape=jax.ShapeDtypeStruct((kinds, rows, width), jnp.float32),
        input_output_aliases=aliases,
        compiler_params=pltpu.CompilerParams(vmem_limit_bytes=VMEM),
        cost_estimate=pl.CostEstimate(
            flops=2 * kinds * rows * depth * width,
            bytes_accessed=2 * kinds * depth * width + 8 * kinds * rows * width,
            transcendentals=0,
        ),
    )(*args)


def head_norm(values, gain):
    average = jnp.mean(values, axis=-1, keepdims=True)
    centred = values - average
    variance = jnp.mean(centred * centred, axis=-1, keepdims=True)
    return (centred * lax.rsqrt(variance + EPS) * gain).astype(jnp.bfloat16)


def attend(projected, gains, block_col, block_row, first, heads, reach):
    _, rows, width = projected.shape
    tile = pick(rows, 256)
    scale = 1.0 / math.sqrt(HEAD_DIM)

    def kernel(q_ref, k_ref, v_ref, gain_ref, col_ref, row_ref, out_ref):
        query = head_norm(q_ref[...], gain_ref[0:1, :])
        key = head_norm(k_ref[...], gain_ref[1:2, :])
        value = v_ref[...].astype(jnp.bfloat16)
        for begin in range(0, rows, tile):
            low = max(0, (begin - reach) // 128 * 128)
            high = min(rows, -(-(begin + tile + reach) // 128) * 128)
            scores = lax.dot_general(
                query[begin : begin + tile],
                key[low:high],
                (((1,), (1,)), ((), ())),
                preferred_element_type=jnp.float32,
            )
            same = col_ref[begin : begin + tile, :] == row_ref[:, low:high]
            scores = jnp.where(same, scores * scale, NEG)
            top = jnp.max(scores, axis=-1, keepdims=True)
            expo = jnp.exp(scores - top)
            total = jnp.sum(expo, axis=-1, keepdims=True)
            weights = (expo * (1.0 / total)).astype(jnp.bfloat16)
            context = jnp.dot(weights, value[low:high], preferred_element_type=jnp.float32)
            out_ref[begin : begin + tile, :] = context.astype(jnp.bfloat16)

    def part(c):
        return pl.BlockSpec((None, rows, HEAD_DIM), lambda h: (c, 0, first + h))

    return pl.pallas_call(
        kernel,
        grid=(heads,),
        in_specs=[
            part(0),
            part(1),
            part(2),
            pl.BlockSpec((None, 2, HEAD_DIM), lambda h: (first + h, 0, 0)),
            pl.BlockSpec((rows, 1), lambda h: (0, 0)),
            pl.BlockSpec((1, rows), lambda h: (0, 0)),
        ],
        out_specs=pl.BlockSpec((rows, HEAD_DIM), lambda h: (0, h)),
        out_shape=jax.ShapeDtypeStruct((rows, heads * HEAD_DIM), jnp.bfloat16),
        compiler_params=pltpu.CompilerParams(vmem_limit_bytes=VMEM),
        cost_estimate=pl.CostEstimate(
            flops=4 * heads * rows * rows * HEAD_DIM,
            bytes_accessed=14 * heads * rows * HEAD_DIM,
            transcendentals=heads * rows * rows,
        ),
    )(projected, projected, projected, gains, block_col, block_row)


def project_out(parts, weight, which, acc, residual):
    rows = parts[0].shape[0]
    _, depth, width = weight.shape
    cols = pick(width, 512)
    count = len(parts)

    def kernel(which_ref, *refs):
        out_ref = refs[-1]
        w_ref = refs[count]
        begin = 0
        total = None if acc is None else refs[count + 1][...]
        for x_ref in refs[:count]:
            depth_of = x_ref.shape[1]
            part = jnp.dot(
                x_ref[...], w_ref[begin : begin + depth_of, :], preferred_element_type=jnp.float32
            )
            total = part if total is None else total + part
            begin += depth_of
        if residual is not None:
            total = refs[-2][...].astype(jnp.float32) + total
        out_ref[...] = total.astype(out_ref.dtype)

    tile = pl.BlockSpec((rows, cols), lambda j, w: (0, j))
    in_specs = [pl.BlockSpec(p.shape, lambda j, w: (0, 0)) for p in parts]
    in_specs.append(pl.BlockSpec((None, depth, cols), lambda j, w: (w[0], 0, j)))
    args = [jnp.reshape(which, (1,)), *parts, weight]
    for extra in (acc, residual):
        if extra is not None:
            in_specs.append(tile)
            args.append(extra)
    out_type = jnp.float32 if residual is None else jnp.bfloat16
    return pl.pallas_call(
        kernel,
        grid_spec=pltpu.PrefetchScalarGridSpec(
            num_scalar_prefetch=1, grid=(width // cols,), in_specs=in_specs, out_specs=tile
        ),
        out_shape=jax.ShapeDtypeStruct((rows, width), out_type),
        compiler_params=pltpu.CompilerParams(vmem_limit_bytes=VMEM),
        cost_estimate=pl.CostEstimate(
            flops=2 * rows * depth * width,
            bytes_accessed=2 * depth * width + 8 * rows * width,
            transcendentals=0,
        ),
    )(*args)


def exchange_out_weight(out_weight, n, groups):
    depth, features = out_weight.shape
    place = lax.axis_index("mp")
    piece = depth // groups
    cols = features // n
    mine = lax.dynamic_slice_in_dim(out_weight, lax.axis_index("dp") * piece, piece, axis=0)

    def columns(index):
        return lax.dynamic_slice_in_dim(mine, index * cols, cols, axis=1)

    pieces = jnp.zeros((n, piece, cols), out_weight.dtype)
    pieces = lax.dynamic_update_slice_in_dim(pieces, columns(place)[None], place, axis=0)
    for d in range(1, n):
        sent = lax.ppermute(
            columns((place + d) % n), "mp", [(i, (i + d) % n) for i in range(n)]
        )
        pieces = lax.dynamic_update_slice_in_dim(pieces, sent[None], (place - d) % n, axis=0)
    return lax.all_gather(pieces, "dp", axis=1, tiled=True)


def shards(tokens, dest_pos, src_row, segment_ids, norm_gain, qkv_weight, qk_gain, out_weight):
    groups = lax.axis_size("dp")
    n = lax.axis_size("mp")
    place = lax.axis_index("mp")
    rows, cols = tokens.shape
    features = cols * n
    reach = 3 * rows // (2 * groups)
    heads = qkv_weight.shape[2] // HEAD_DIM

    segment = lax.all_gather(segment_ids, "dp", tiled=True)[dest_pos]
    block = dest_pos // rows * groups + segment
    block_col = block[:, None]
    block_row = block[None, :]
    gains = jnp.transpose(qk_gain, (1, 0, 2))

    with jax.named_scope("moments"):
        values = tokens.astype(jnp.float32)
        moments = lax.psum((jnp.sum(values, axis=1), jnp.sum(values * values, axis=1)), "mp")
        average = moments[0] / features
        inverse = lax.rsqrt(moments[1] / features - average * average + EPS)

    arrived = relay(tokens, "mp", n)
    sources = origins("mp", n)
    out_columns = exchange_out_weight(out_weight, n, groups)

    def normalize(block, origin):
        gain = lax.dynamic_slice_in_dim(norm_gain, origin * cols, cols)
        centred = block.astype(jnp.float32) - average[:, None]
        return (centred * inverse[:, None] * gain).astype(jnp.bfloat16)

    projected = None
    for block, origin in zip([tokens] + arrived, [place] + sources):
        with jax.named_scope("project"):
            projected = project(normalize(block, origin), qkv_weight, origin, projected)

    chunk = 2 if heads % 2 == 0 else 1
    contexts = []
    for first in range(0, heads, chunk):
        with jax.named_scope("attend"):
            contexts.append(
                attend(projected, gains, block_col, block_row, first, chunk, reach)
            )
    moved = [relay(context, "mp", n) for context in contexts]

    total = project_out(contexts, out_columns, place, None, None)
    for k in range(n - 1):
        last = k == n - 2
        total = project_out(
            [m[k] for m in moved], out_columns, sources[k], total, tokens if last else None
        )
    return total


def solution(mesh):
    in_specs = (
        P("dp", "mp"),
        P("dp"),
        P("dp"),
        P("dp"),
        P(),
        P(None, None, "mp"),
        P(None, "mp", None),
        P("mp", None),
    )
    out_specs = P("dp", "mp")
    return jax.shard_map(shards, mesh=mesh, in_specs=in_specs, out_specs=out_specs, check_vma=False)
```

```python
import functools
import math

import jax
import jax.numpy as jnp
import numpy as np
from jax import lax
from jax.experimental import pallas as pl
from jax.experimental.pallas import tpu as pltpu
from jax.sharding import PartitionSpec as P

HEAD_DIM = 128
EPS = 1e-06
NEG = -1e30
VMEM = 56 * 1024 * 1024
COST = pl.CostEstimate(flops=1024, bytes_accessed=1024, transcendentals=0)


def pick(total, wanted):
    return max(w for w in range(128, min(total, wanted) + 1, 128) if total % w == 0)


def line_schedule(n):
    steps = {}
    for s in range(1, n):
        for kind, low in (("E", 0), ("O", 1)):
            pairs = []
            for i in range(low, n - 1, 2):
                if i - s + 1 >= 0:
                    pairs.append((i, i + 1))
                if i + s <= n - 1:
                    pairs.append((i + 1, i))
            if pairs:
                steps[(s, kind)] = pairs
    slots = [[] for _ in range(n)]
    for (s, kind), pairs in sorted(steps.items()):
        for source, target in pairs:
            origin = target - s if source < target else target + s
            slots[target].append(((s, kind), origin))
    return steps, slots


class Relay:
    def __init__(self, block, axis, n):
        self.axis, self.n = axis, n
        self.steps, self.slots = line_schedule(n)
        self.got = {(0, "E"): block, (0, "O"): block}

    def step(self, s, *after):
        kinds = [kind for kind in "EO" if (s, kind) in self.steps]
        sources = [self.got[(s - 1, "O" if kind == "E" else "E")] for kind in kinds]
        sources = lax.optimization_barrier((*sources, *after))
        for kind, source in zip(kinds, sources):
            self.got[(s, kind)] = lax.ppermute(source, self.axis, self.steps[(s, kind)])

    def arrived(self, k):
        keys = sorted({slot[k][0] for slot in self.slots})
        if all({key for key, _ in slot} & set(keys) == {slot[k][0]} for slot in self.slots):
            return [self.got[key] for key in keys]
        place = lax.axis_index(self.axis)
        value = self.got[keys[0]]
        for key in keys[1:]:
            here = np.array([slot[k][0] == key for slot in self.slots])
            value = jnp.where(jnp.asarray(here)[place], self.got[key], value)
        return [value]


def origins(axis, n):
    _, slots = line_schedule(n)
    table = np.array([[slots[i][k][1] for k in range(n - 1)] for i in range(n)], np.int32)
    place = lax.axis_index(axis)
    return [jnp.asarray(table)[place, k] for k in range(n - 1)]


def whole(refs):
    value = refs[0][...]
    for ref in refs[1:]:
        value = value + ref[...]
    return value


def project(parts, weight, which, acc):
    rows, depth = parts[0].shape
    kinds, _, width = weight.shape
    cols = pick(width, 768)
    count = len(parts)

    def kernel(which_ref, *refs):
        x = whole(refs[:count])
        part = jnp.dot(x, refs[count][...], preferred_element_type=jnp.float32)
        if acc is not None:
            part = part + refs[count + 1][...]
        refs[-1][...] = part

    tile = pl.BlockSpec((None, rows, cols), lambda c, j, w: (c, 0, j))
    in_specs = [pl.BlockSpec((rows, depth), lambda c, j, w: (0, 0)) for _ in parts]
    in_specs.append(pl.BlockSpec((None, depth, cols), lambda c, j, w: (c, w[0], j)))
    args = [jnp.reshape(which, (1,)), *parts, weight]
    aliases = {}
    if acc is not None:
        in_specs.append(tile)
        args.append(acc)
        aliases = {count + 2: 0}
    return pl.pallas_call(
        kernel,
        grid_spec=pltpu.PrefetchScalarGridSpec(
            num_scalar_prefetch=1,
            grid=(kinds, width // cols),
            in_specs=in_specs,
            out_specs=tile,
        ),
        out_shape=jax.ShapeDtypeStruct((kinds, rows, width), jnp.float32),
        input_output_aliases=aliases,
        compiler_params=pltpu.CompilerParams(vmem_limit_bytes=VMEM),
        cost_estimate=pl.CostEstimate(
            flops=2 * kinds * rows * depth * width,
            bytes_accessed=2 * kinds * depth * width + 8 * kinds * rows * width,
            transcendentals=0,
        ),
    )(*args)


def head_norm(values, gain):
    average = jnp.mean(values, axis=-1, keepdims=True)
    centred = values - average
    variance = jnp.mean(centred * centred, axis=-1, keepdims=True)
    return (centred * lax.rsqrt(variance + EPS) * gain).astype(jnp.bfloat16)


def attend(parts, weight, which, acc, gains, block_col, block_row, first, heads, reach):
    rows, depth = parts[0].shape
    kinds = weight.shape[0]
    cols = heads * HEAD_DIM
    deep = pick(depth, 512)
    steps = depth // deep
    tile = pick(rows, 256)
    scale = 1.0 / math.sqrt(HEAD_DIM)
    count = len(parts)

    def one_head(q, k, v, gain, col_ref, row_ref, out_ref, place):
        query = head_norm(q, gain[0:1, :])
        key = head_norm(k, gain[1:2, :])
        value = v.astype(jnp.bfloat16)
        for begin in range(0, rows, tile):
            low = max(0, (begin - reach) // 128 * 128)
            high = min(rows, -(-(begin + tile + reach) // 128) * 128)
            scores = lax.dot_general(
                query[begin : begin + tile],
                key[low:high],
                (((1,), (1,)), ((), ())),
                preferred_element_type=jnp.float32,
            )
            same = col_ref[begin : begin + tile, :] == row_ref[:, low:high]
            scores = jnp.where(same, scores * scale, NEG)
            top = jnp.max(scores, axis=-1, keepdims=True)
            expo = jnp.exp(scores - top)
            total = jnp.sum(expo, axis=-1, keepdims=True)
            weights = (expo * (1.0 / total)).astype(jnp.bfloat16)
            context = jnp.dot(weights, value[low:high], preferred_element_type=jnp.float32)
            out_ref[begin : begin + tile, place : place + HEAD_DIM] = context.astype(jnp.bfloat16)

    def kernel(which_ref, *refs):
        x_refs = refs[:count]
        w_refs = refs[count : count + kinds]
        acc_refs = refs[count + kinds : count + 2 * kinds]
        gain_ref, col_ref, row_ref, out_ref, held = refs[count + 2 * kinds :]
        step = pl.program_id(0)
        x = whole(x_refs)

        @pl.when(step == 0)
        def _():
            for c in range(kinds):
                held[c] = acc_refs[c][...] + jnp.dot(
                    x, w_refs[c][...], preferred_element_type=jnp.float32
                )

        @pl.when(step > 0)
        def _():
            for c in range(kinds):
                held[c] += jnp.dot(x, w_refs[c][...], preferred_element_type=jnp.float32)

        @pl.when(step == steps - 1)
        def _():
            for h in range(heads):
                at = slice(h * HEAD_DIM, (h + 1) * HEAD_DIM)
                one_head(
                    held[0, :, at], held[1, :, at], held[2, :, at], gain_ref[h],
                    col_ref, row_ref, out_ref, h * HEAD_DIM,
                )

    def w_spec(c):
        return pl.BlockSpec(
            (None, deep, cols), lambda s, w: (c, w[0] * steps + s, first // heads)
        )

    def acc_spec(c):
        return pl.BlockSpec((None, rows, cols), lambda s, w: (c, 0, first // heads))

    in_specs = [pl.BlockSpec((rows, deep), lambda s, w: (0, s)) for _ in parts]
    in_specs += [w_spec(c) for c in range(kinds)] + [acc_spec(c) for c in range(kinds)]
    in_specs += [
        pl.BlockSpec((heads, 2, HEAD_DIM), lambda s, w: (first // heads, 0, 0)),
        pl.BlockSpec((rows, 1), lambda s, w: (0, 0)),
        pl.BlockSpec((1, rows), lambda s, w: (0, 0)),
    ]
    return pl.pallas_call(
        kernel,
        grid_spec=pltpu.PrefetchScalarGridSpec(
            num_scalar_prefetch=1,
            grid=(steps,),
            in_specs=in_specs,
            out_specs=pl.BlockSpec((rows, cols), lambda s, w: (0, 0)),
            scratch_shapes=[pltpu.VMEM((kinds, rows, cols), jnp.float32)],
        ),
        out_shape=jax.ShapeDtypeStruct((rows, cols), jnp.bfloat16),
        compiler_params=pltpu.CompilerParams(vmem_limit_bytes=VMEM),
        cost_estimate=COST,
    )(
        jnp.reshape(which, (1,)), *parts, *([weight] * kinds), *([acc] * kinds),
        gains, block_col, block_row,
    )


def project_out(pieces, weight, which, acc, residual):
    rows = pieces[0][0].shape[0]
    depth = sum(piece[0].shape[1] for piece in pieces)
    width = which[1]
    above = which[3] // depth
    high = pick(rows, 256)
    flat = [array for piece in pieces for array in piece]

    def kernel(which_ref, *refs):
        out_ref = refs[-1]
        w_ref = refs[len(flat)]
        total = None if acc is None else refs[len(flat) + 1][...]
        first = begin = 0
        for piece in pieces:
            x = whole(refs[first : first + len(piece)])
            first += len(piece)
            part = jnp.dot(
                x, w_ref[begin : begin + x.shape[1], :], preferred_element_type=jnp.float32
            )
            begin += x.shape[1]
            total = part if total is None else total + part
        if residual is not None:
            total = refs[-2][...].astype(jnp.float32) + total
        out_ref[...] = total.astype(out_ref.dtype)

    tile = pl.BlockSpec((high, width), lambda i, w: (i, 0))
    in_specs = [pl.BlockSpec((high, p.shape[1]), lambda i, w: (i, 0)) for p in flat]
    in_specs.append(pl.BlockSpec((None, depth, width), lambda i, w: (w[0], above, w[1])))
    args = [jnp.stack([which[0], which[2]]), *flat, weight]
    for extra in (acc, residual):
        if extra is not None:
            in_specs.append(tile)
            args.append(extra)
    out_type = jnp.float32 if residual is None else jnp.bfloat16
    return pl.pallas_call(
        kernel,
        grid_spec=pltpu.PrefetchScalarGridSpec(
            num_scalar_prefetch=1, grid=(rows // high,), in_specs=in_specs, out_specs=tile
        ),
        out_shape=jax.ShapeDtypeStruct((rows, width), out_type),
        compiler_params=pltpu.CompilerParams(vmem_limit_bytes=VMEM),
        cost_estimate=COST,
    )(*args)


def exchange_out_weight(out_weight, n, groups):
    depth, features = out_weight.shape
    place = lax.axis_index("mp")
    piece = depth // groups
    cols = features // n
    mine = lax.dynamic_slice_in_dim(out_weight, lax.axis_index("dp") * piece, piece, axis=0)

    def columns(index):
        return lax.dynamic_slice_in_dim(mine, index * cols, cols, axis=1)

    received = [(place, columns(place))]
    for d in range(1, n):
        sent = lax.ppermute(
            columns((place + d) % n), "mp", [(i, (i + d) % n) for i in range(n)]
        )
        received.append(((place - d) % n, sent))
    return received


def gather_out_weight(received, after):
    arrays = lax.optimization_barrier((*[array for _, array in received], after))[:-1]
    pieces = jnp.zeros((len(arrays), *arrays[0].shape), arrays[0].dtype)
    for (origin, _), array in zip(received, arrays):
        pieces = lax.dynamic_update_slice_in_dim(pieces, array[None], origin, axis=0)
    return lax.all_gather(pieces, "dp", axis=1, tiled=True)


def shards(tokens, dest_pos, src_row, segment_ids, norm_gain, qkv_weight, qk_gain, out_weight):
    groups = lax.axis_size("dp")
    n = lax.axis_size("mp")
    place = lax.axis_index("mp")
    rows, cols = tokens.shape
    features = cols * n
    reach = 3 * rows // (2 * groups)
    heads = qkv_weight.shape[2] // HEAD_DIM

    segment = lax.all_gather(segment_ids, "dp", tiled=True)[dest_pos]
    block = dest_pos // rows * groups + segment
    block_col = block[:, None]
    block_row = block[None, :]
    gains = jnp.transpose(qk_gain, (1, 0, 2))

    with jax.named_scope("normalize"):
        values = tokens.astype(jnp.float32)
        moments = lax.psum((jnp.sum(values, axis=1), jnp.sum(values * values, axis=1)), "mp")
        average = moments[0] / features
        variance = moments[1] / features - average * average
        gain = lax.dynamic_slice_in_dim(norm_gain, place * cols, cols)
        centred = values - average[:, None]
        normed = (centred * lax.rsqrt(variance + EPS)[:, None] * gain).astype(jnp.bfloat16)

    sources = origins("mp", n)

    def step_project(parts, origin, acc):
        with jax.named_scope("project"):
            return project(parts, qkv_weight, origin, acc)

    line = Relay(normed, "mp", n)
    line.step(1)
    projected = step_project([normed], place, None)
    for s in range(2, n):
        line.step(s, projected, block)
        projected = step_project(line.arrived(s - 2), sources[s - 2], projected)
    last = line.arrived(n - 2)
    after = lax.optimization_barrier((out_weight, projected, *last))
    received = exchange_out_weight(after[0], n, groups)

    chunk = 2 if heads % 2 == 0 else 1
    contexts, lines = [], []
    for first in range(0, heads, chunk):
        if contexts:
            gains, _ = lax.optimization_barrier((gains, contexts[-1]))
        with jax.named_scope("attend"):
            context = attend(
                last, qkv_weight, sources[n - 2], projected, gains, block_col, block_row,
                first, chunk, reach,
            )
        contexts.append(context)
        lines.append(Relay(context, "mp", n))
        lines[-1].step(1)
    out_columns = gather_out_weight(received, contexts[min(1, len(contexts) - 1)])

    zero = jnp.zeros((), jnp.int32)

    def step_out(k, acc, residual, first, end):
        pieces = [line.arrived(k) for line in lines[first:end]]
        where = (sources[k], cols, zero, first * chunk * HEAD_DIM)
        return project_out(pieces, out_columns, where, acc, residual)

    total = project_out(
        [[c] for c in contexts], out_weight[None], (zero, cols, place, 0), None, None
    )
    count = len(lines)
    for s in range(2, n):
        for line in lines[:-1]:
            line.step(s)
        lines[-1].step(s, total)
        total = step_out(s - 2, total, None, 0, count)
    total = step_out(n - 2, total, None, 0, count - 1)
    return step_out(n - 2, total, tokens, count - 1, count)


def solution(mesh):
    in_specs = (
        P("dp", "mp"),
        P("dp"),
        P("dp"),
        P("dp"),
        P(),
        P(None, None, "mp"),
        P(None, "mp", None),
        P("mp", None),
    )
    out_specs = P("dp", "mp")
    return jax.shard_map(shards, mesh=mesh, in_specs=in_specs, out_specs=out_specs, check_vma=False)
```

```python
import functools
import math

import jax
import jax.numpy as jnp
import numpy as np
from jax import lax
from jax.experimental import pallas as pl
from jax.experimental.pallas import tpu as pltpu
from jax.sharding import PartitionSpec as P

HEAD_DIM = 128
EPS = 1e-06
NEG = -1e30
VMEM = 56 * 1024 * 1024
COST = pl.CostEstimate(flops=15 * 10**9, bytes_accessed=2**20, transcendentals=0)


def pick(total, wanted):
    return max(w for w in range(128, min(total, wanted) + 1, 128) if total % w == 0)


def line_schedule(n):
    steps = {}
    for s in range(1, n):
        for kind, low in (("E", 0), ("O", 1)):
            pairs = []
            for i in range(low, n - 1, 2):
                if i - s + 1 >= 0:
                    pairs.append((i, i + 1))
                if i + s <= n - 1:
                    pairs.append((i + 1, i))
            if pairs:
                steps[(s, kind)] = pairs
    slots = [[] for _ in range(n)]
    for (s, kind), pairs in sorted(steps.items()):
        for source, target in pairs:
            origin = target - s if source < target else target + s
            slots[target].append(((s, kind), origin))
    return steps, slots


class Relay:
    def __init__(self, block, axis, n):
        self.axis, self.n = axis, n
        self.steps, self.slots = line_schedule(n)
        self.got = {(0, "E"): block, (0, "O"): block}

    def step(self, s, *after):
        kinds = [kind for kind in "EO" if (s, kind) in self.steps]
        sources = [self.got[(s - 1, "O" if kind == "E" else "E")] for kind in kinds]
        tied = lax.optimization_barrier((*sources, *after))
        for kind, source in zip(kinds, tied):
            self.got[(s, kind)] = lax.ppermute(source, self.axis, self.steps[(s, kind)])
        return tied[len(kinds) : len(kinds) + len(after)]

    def arrived(self, k):
        keys = sorted({slot[k][0] for slot in self.slots})
        if all({key for key, _ in slot} & set(keys) == {slot[k][0]} for slot in self.slots):
            return [self.got[key] for key in keys]
        place = lax.axis_index(self.axis)
        value = self.got[keys[0]]
        for key in keys[1:]:
            here = np.array([slot[k][0] == key for slot in self.slots])
            value = jnp.where(jnp.asarray(here)[place], self.got[key], value)
        return [value]


def origins(axis, n):
    _, slots = line_schedule(n)
    table = np.array([[slots[i][k][1] for k in range(n - 1)] for i in range(n)], np.int32)
    place = lax.axis_index(axis)
    return [jnp.asarray(table)[place, k] for k in range(n - 1)]


def whole(refs):
    value = refs[0][...]
    for ref in refs[1:]:
        value = value + ref[...]
    return value


def normalize(refs, average_ref, inverse_ref, gain_ref):
    centred = whole(refs).astype(jnp.float32) - average_ref[...]
    return (centred * inverse_ref[...] * gain_ref[...]).astype(jnp.bfloat16)


def project(parts, norm, weight, which, acc):
    rows, depth = parts[0].shape
    kinds, _, width = weight.shape
    cols = pick(width, 768)
    count = len(parts)

    def kernel(which_ref, *refs):
        normed, out_ref = refs[-1], refs[-2]

        @pl.when((pl.program_id(0) == 0) & (pl.program_id(1) == 0))
        def _():
            normed[...] = normalize(refs[:count], *refs[count : count + 3])

        part = jnp.dot(normed[...], refs[count + 3][...], preferred_element_type=jnp.float32)
        if acc is not None:
            part = part + refs[count + 4][...]
        out_ref[...] = part

    tile = pl.BlockSpec((None, rows, cols), lambda c, j, w: (c, 0, j))
    in_specs = [pl.BlockSpec((rows, depth), lambda c, j, w: (0, 0)) for _ in parts]
    in_specs += [pl.BlockSpec((rows, 1), lambda c, j, w: (0, 0))] * 2
    in_specs.append(pl.BlockSpec((1, depth), lambda c, j, w: (0, w[0])))
    in_specs.append(pl.BlockSpec((None, depth, cols), lambda c, j, w: (c, w[0], j)))
    args = [jnp.reshape(which, (1,)), *parts, *norm, weight]
    aliases = {}
    if acc is not None:
        in_specs.append(tile)
        args.append(acc)
        aliases = {len(args) - 1: 0}
    return pl.pallas_call(
        kernel,
        grid_spec=pltpu.PrefetchScalarGridSpec(
            num_scalar_prefetch=1,
            grid=(kinds, width // cols),
            in_specs=in_specs,
            out_specs=tile,
            scratch_shapes=[pltpu.VMEM((rows, depth), jnp.bfloat16)],
        ),
        out_shape=jax.ShapeDtypeStruct((kinds, rows, width), jnp.float32),
        input_output_aliases=aliases,
        compiler_params=pltpu.CompilerParams(vmem_limit_bytes=VMEM),
        cost_estimate=pl.CostEstimate(
            flops=2 * kinds * rows * depth * width,
            bytes_accessed=2 * kinds * depth * width + 8 * kinds * rows * width,
            transcendentals=0,
        ),
    )(*args)


def head_norm(values, gain):
    average = jnp.mean(values, axis=-1, keepdims=True)
    centred = values - average
    variance = jnp.mean(centred * centred, axis=-1, keepdims=True)
    return (centred * lax.rsqrt(variance + EPS) * gain).astype(jnp.bfloat16)


def attend(parts, norm, weight, which, acc, gains, block_col, block_row, first, heads, reach):
    rows, depth = parts[0].shape
    kinds = weight.shape[0]
    cols = heads * HEAD_DIM
    deep = pick(depth, 512)
    steps = depth // deep
    tile = pick(rows, 256)
    scale = 1.0 / math.sqrt(HEAD_DIM)
    count = len(parts)

    def one_head(q, k, v, gain, col_ref, row_ref, out_ref, place):
        query = head_norm(q, gain[0:1, :])
        key = head_norm(k, gain[1:2, :])
        value = v.astype(jnp.bfloat16)
        for begin in range(0, rows, tile):
            low = max(0, (begin - reach) // 128 * 128)
            high = min(rows, -(-(begin + tile + reach) // 128) * 128)
            scores = lax.dot_general(
                query[begin : begin + tile],
                key[low:high],
                (((1,), (1,)), ((), ())),
                preferred_element_type=jnp.float32,
            )
            same = col_ref[begin : begin + tile, :] == row_ref[:, low:high]
            scores = jnp.where(same, scores * scale, NEG)
            top = jnp.max(scores, axis=-1, keepdims=True)
            expo = jnp.exp(scores - top)
            total = jnp.sum(expo, axis=-1, keepdims=True)
            weights = (expo * (1.0 / total)).astype(jnp.bfloat16)
            context = jnp.dot(weights, value[low:high], preferred_element_type=jnp.float32)
            out_ref[begin : begin + tile, place : place + HEAD_DIM] = context.astype(jnp.bfloat16)

    def kernel(which_ref, *refs):
        norm_refs = refs[count : count + 3]
        x_refs, refs = refs[:count], refs[3:]
        w_refs = refs[count : count + kinds]
        acc_refs = refs[count + kinds : count + 2 * kinds]
        gain_ref, col_ref, row_ref, out_ref, held = refs[count + 2 * kinds :]
        step = pl.program_id(0)
        x = normalize(x_refs, *norm_refs)

        @pl.when(step == 0)
        def _():
            for c in range(kinds):
                held[c] = acc_refs[c][...] + jnp.dot(
                    x, w_refs[c][...], preferred_element_type=jnp.float32
                )

        @pl.when(step > 0)
        def _():
            for c in range(kinds):
                held[c] += jnp.dot(x, w_refs[c][...], preferred_element_type=jnp.float32)

        @pl.when(step == steps - 1)
        def _():
            for h in range(heads):
                at = slice(h * HEAD_DIM, (h + 1) * HEAD_DIM)
                one_head(
                    held[0, :, at], held[1, :, at], held[2, :, at], gain_ref[h],
                    col_ref, row_ref, out_ref, h * HEAD_DIM,
                )

    def w_spec(c):
        return pl.BlockSpec(
            (None, deep, cols), lambda s, w: (c, w[0] * steps + s, first // heads)
        )

    def acc_spec(c):
        return pl.BlockSpec((None, rows, cols), lambda s, w: (c, 0, first // heads))

    in_specs = [pl.BlockSpec((rows, deep), lambda s, w: (0, s)) for _ in parts]
    in_specs += [pl.BlockSpec((rows, 1), lambda s, w: (0, 0))] * 2
    in_specs.append(pl.BlockSpec((1, deep), lambda s, w: (0, w[0] * steps + s)))
    in_specs += [w_spec(c) for c in range(kinds)] + [acc_spec(c) for c in range(kinds)]
    in_specs += [
        pl.BlockSpec((heads, 2, HEAD_DIM), lambda s, w: (first // heads, 0, 0)),
        pl.BlockSpec((rows, 1), lambda s, w: (0, 0)),
        pl.BlockSpec((1, rows), lambda s, w: (0, 0)),
    ]
    return pl.pallas_call(
        kernel,
        grid_spec=pltpu.PrefetchScalarGridSpec(
            num_scalar_prefetch=1,
            grid=(steps,),
            in_specs=in_specs,
            out_specs=pl.BlockSpec((rows, cols), lambda s, w: (0, 0)),
            scratch_shapes=[pltpu.VMEM((kinds, rows, cols), jnp.float32)],
        ),
        out_shape=jax.ShapeDtypeStruct((rows, cols), jnp.bfloat16),
        compiler_params=pltpu.CompilerParams(vmem_limit_bytes=VMEM),
        cost_estimate=COST,
    )(
        jnp.reshape(which, (1,)), *parts, *norm, *([weight] * kinds), *([acc] * kinds),
        gains, block_col, block_row,
    )


def project_out(pieces, weight, which, acc, residual):
    rows = pieces[0][0].shape[0]
    _, depth, _ = weight.shape
    width = which[1]
    high = pick(rows, 256)
    flat = [array for piece in pieces for array in piece]

    def kernel(which_ref, *refs):
        out_ref = refs[-1]
        w_ref = refs[len(flat)]
        total = None if acc is None else refs[len(flat) + 1][...]
        first = begin = 0
        for piece in pieces:
            x = whole(refs[first : first + len(piece)])
            first += len(piece)
            part = jnp.dot(
                x, w_ref[begin : begin + x.shape[1], :], preferred_element_type=jnp.float32
            )
            begin += x.shape[1]
            total = part if total is None else total + part
        if residual is not None:
            total = refs[-2][...].astype(jnp.float32) + total
        out_ref[...] = total.astype(out_ref.dtype)

    tile = pl.BlockSpec((high, width), lambda i, w: (i, 0))
    in_specs = [pl.BlockSpec((high, p.shape[1]), lambda i, w: (i, 0)) for p in flat]
    in_specs.append(pl.BlockSpec((None, depth, width), lambda i, w: (w[0], 0, w[1])))
    args = [jnp.stack([which[0], which[2]]), *flat, weight]
    for extra in (acc, residual):
        if extra is not None:
            in_specs.append(tile)
            args.append(extra)
    out_type = jnp.float32 if residual is None else jnp.bfloat16
    return pl.pallas_call(
        kernel,
        grid_spec=pltpu.PrefetchScalarGridSpec(
            num_scalar_prefetch=1, grid=(rows // high,), in_specs=in_specs, out_specs=tile
        ),
        out_shape=jax.ShapeDtypeStruct((rows, width), out_type),
        compiler_params=pltpu.CompilerParams(vmem_limit_bytes=VMEM),
        cost_estimate=COST,
    )(*args)


def exchange_out_weight(out_weight, n, groups):
    depth, features = out_weight.shape
    place = lax.axis_index("mp")
    piece = depth // groups
    cols = features // n
    mine = lax.dynamic_slice_in_dim(out_weight, lax.axis_index("dp") * piece, piece, axis=0)

    def columns(index):
        return lax.dynamic_slice_in_dim(mine, index * cols, cols, axis=1)

    received = [(place, columns(place))]
    for d in range(1, n):
        sent = lax.ppermute(
            columns((place + d) % n), "mp", [(i, (i + d) % n) for i in range(n)]
        )
        received.append(((place - d) % n, sent))
    return received


def stack(received):
    pieces = jnp.zeros((len(received), *received[0][1].shape), received[0][1].dtype)
    for origin, array in received:
        pieces = lax.dynamic_update_slice_in_dim(pieces, array[None], origin, axis=0)
    return pieces


def shards(tokens, dest_pos, src_row, segment_ids, norm_gain, qkv_weight, qk_gain, out_weight):
    groups = lax.axis_size("dp")
    n = lax.axis_size("mp")
    place = lax.axis_index("mp")
    rows, cols = tokens.shape
    features = cols * n
    reach = 3 * rows // (2 * groups)
    heads = qkv_weight.shape[2] // HEAD_DIM

    segment = lax.all_gather(segment_ids, "dp", tiled=True)[dest_pos]
    block = dest_pos // rows * groups + segment
    block_col = block[:, None]
    block_row = block[None, :]
    gains = jnp.transpose(qk_gain, (1, 0, 2))

    with jax.named_scope("moments"):
        values = tokens.astype(jnp.float32)
        moments = jnp.stack([jnp.sum(values, axis=1), jnp.sum(values * values, axis=1)])
        sums = moments
        for d in range(1, n):
            sums = sums + lax.ppermute(moments, "mp", [(i, (i + d) % n) for i in range(n)])
        average = sums[0] / features
        variance = sums[1] / features - average * average
        inverse = lax.rsqrt(variance + EPS)
        norm = (average[:, None], inverse[:, None], norm_gain[None, :])

    sources = origins("mp", n)

    def step_project(parts, origin, acc):
        with jax.named_scope("project"):
            return project(parts, norm, qkv_weight, origin, acc)

    line = Relay(tokens, "mp", n)
    line.step(1, sums)
    projected = step_project([tokens], place, None)
    pieces = out_weight
    for s in range(2, n):
        there = [line.got[key] for key in line.steps if key[0] == s - 1]
        pieces = line.step(s, projected, block, pieces, *there)[2]
        if s == 2:
            pieces = stack(exchange_out_weight(pieces, n, groups))
        elif s == 3:
            out_columns = lax.all_gather(pieces, "dp", axis=1, tiled=True)
        projected = step_project(line.arrived(s - 2), sources[s - 2], projected)
    last = line.arrived(n - 2)

    chunk = 2 if heads % 2 == 0 else 1
    contexts, lines = [], []
    for first in range(0, heads, chunk):
        if contexts:
            before = [contexts[-1]]
            if len(lines) >= 2:
                before += [lines[-2].got[(1, kind)] for kind in "EO"]
            gains = lax.optimization_barrier((gains, *before))[0]
        with jax.named_scope("attend"):
            context = attend(
                last, norm, qkv_weight, sources[n - 2], projected, gains, block_col, block_row,
                first, chunk, reach,
            )
        contexts.append(context)
        lines.append(Relay(context, "mp", n))
        lines[-1].step(1)

    zero = jnp.zeros((), jnp.int32)

    def step_out(k, acc, residual):
        pieces = [line.arrived(k) for line in lines]
        return project_out(pieces, out_columns, (sources[k], cols, zero), acc, residual)

    lines[0].step(2)
    there = [lines[0].got[key] for key in lines[0].steps if key[0] == 2]
    tied = lax.optimization_barrier((*contexts, *there))[: len(contexts)]
    total = project_out([[c] for c in tied], out_weight[None], (zero, cols, place), None, None)
    for s in range(2, n):
        for line in lines:
            if line is lines[-1]:
                line.step(s, total)
            elif s > 2 or line is not lines[0]:
                line.step(s)
        total = step_out(s - 2, total, None)
    return step_out(n - 2, total, tokens)


def solution(mesh):
    in_specs = (
        P("dp", "mp"),
        P("dp"),
        P("dp"),
        P("dp"),
        P(),
        P(None, None, "mp"),
        P(None, "mp", None),
        P("mp", None),
    )
    out_specs = P("dp", "mp")
    return jax.shard_map(shards, mesh=mesh, in_specs=in_specs, out_specs=out_specs, check_vma=False)
```

```python
import functools
import math

import jax
import jax.numpy as jnp
import numpy as np
from jax import lax
from jax.experimental import pallas as pl
from jax.experimental.pallas import tpu as pltpu
from jax.sharding import PartitionSpec as P

HEAD_DIM = 128
EPS = 1e-06
NEG = -1e30
VMEM = 56 * 1024 * 1024
COST = pl.CostEstimate(flops=15 * 10**9, bytes_accessed=2**20, transcendentals=0)


def pick(total, wanted):
    return max(w for w in range(128, min(total, wanted) + 1, 128) if total % w == 0)


def line_schedule(n):
    steps = {}
    for s in range(1, n):
        for kind, low in (("E", 0), ("O", 1)):
            pairs = []
            for i in range(low, n - 1, 2):
                if i - s + 1 >= 0:
                    pairs.append((i, i + 1))
                if i + s <= n - 1:
                    pairs.append((i + 1, i))
            if pairs:
                steps[(s, kind)] = pairs
    slots = [[] for _ in range(n)]
    for (s, kind), pairs in sorted(steps.items()):
        for source, target in pairs:
            origin = target - s if source < target else target + s
            slots[target].append(((s, kind), origin))
    return steps, slots


class Relay:
    def __init__(self, block, axis, n):
        self.axis, self.n = axis, n
        self.steps, self.slots = line_schedule(n)
        self.got = {(0, "E"): block, (0, "O"): block}

    def step(self, s, *after):
        kinds = [kind for kind in "EO" if (s, kind) in self.steps]
        sources = [self.got[(s - 1, "O" if kind == "E" else "E")] for kind in kinds]
        tied = lax.optimization_barrier((*sources, *after))
        for kind, source in zip(kinds, tied):
            self.got[(s, kind)] = lax.ppermute(source, self.axis, self.steps[(s, kind)])
        return tied[len(kinds) : len(kinds) + len(after)]

    def arrived(self, k):
        keys = sorted({slot[k][0] for slot in self.slots})
        if all({key for key, _ in slot} & set(keys) == {slot[k][0]} for slot in self.slots):
            return [self.got[key] for key in keys]
        place = lax.axis_index(self.axis)
        value = self.got[keys[0]]
        for key in keys[1:]:
            here = np.array([slot[k][0] == key for slot in self.slots])
            value = jnp.where(jnp.asarray(here)[place], self.got[key], value)
        return [value]


def origins(axis, n):
    _, slots = line_schedule(n)
    table = np.array([[slots[i][k][1] for k in range(n - 1)] for i in range(n)], np.int32)
    place = lax.axis_index(axis)
    return [jnp.asarray(table)[place, k] for k in range(n - 1)]


def whole(refs):
    value = refs[0][...]
    for ref in refs[1:]:
        value = value + ref[...]
    return value


def normalize(refs, average_ref, inverse_ref, gain_ref):
    centred = whole(refs).astype(jnp.float32) - average_ref[...]
    return (centred * inverse_ref[...] * gain_ref[...]).astype(jnp.bfloat16)


def project(parts, norm, weight, which, acc):
    rows, depth = parts[0].shape
    kinds, _, width = weight.shape
    cols = pick(width, 768)
    count = len(parts)

    def kernel(which_ref, *refs):
        normed, out_ref = refs[-1], refs[-2]

        @pl.when((pl.program_id(0) == 0) & (pl.program_id(1) == 0))
        def _():
            normed[...] = normalize(refs[:count], *refs[count : count + 3])

        part = jnp.dot(normed[...], refs[count + 3][...], preferred_element_type=jnp.float32)
        if acc is not None:
            part = part + refs[count + 4][...]
        out_ref[...] = part

    tile = pl.BlockSpec((None, rows, cols), lambda c, j, w: (c, 0, j))
    in_specs = [pl.BlockSpec((rows, depth), lambda c, j, w: (0, 0)) for _ in parts]
    in_specs += [pl.BlockSpec((rows, 1), lambda c, j, w: (0, 0))] * 2
    in_specs.append(pl.BlockSpec((1, depth), lambda c, j, w: (0, w[0])))
    in_specs.append(pl.BlockSpec((None, depth, cols), lambda c, j, w: (c, w[0], j)))
    args = [jnp.reshape(which, (1,)), *parts, *norm, weight]
    aliases = {}
    if acc is not None:
        in_specs.append(tile)
        args.append(acc)
        aliases = {len(args) - 1: 0}
    return pl.pallas_call(
        kernel,
        grid_spec=pltpu.PrefetchScalarGridSpec(
            num_scalar_prefetch=1,
            grid=(kinds, width // cols),
            in_specs=in_specs,
            out_specs=tile,
            scratch_shapes=[pltpu.VMEM((rows, depth), jnp.bfloat16)],
        ),
        out_shape=jax.ShapeDtypeStruct((kinds, rows, width), jnp.float32),
        input_output_aliases=aliases,
        compiler_params=pltpu.CompilerParams(vmem_limit_bytes=VMEM),
        cost_estimate=pl.CostEstimate(
            flops=2 * kinds * rows * depth * width,
            bytes_accessed=2 * kinds * depth * width + 8 * kinds * rows * width,
            transcendentals=0,
        ),
    )(*args)


def head_norm(values, gain):
    average = jnp.mean(values, axis=-1, keepdims=True)
    centred = values - average
    variance = jnp.mean(centred * centred, axis=-1, keepdims=True)
    return (centred * lax.rsqrt(variance + EPS) * gain).astype(jnp.bfloat16)


def attend(parts, norm, weight, which, acc, gains, block_col, block_row, first, heads, reach):
    rows, depth = parts[0].shape
    kinds = weight.shape[0]
    cols = heads * HEAD_DIM
    deep = pick(depth, 512)
    steps = depth // deep
    tile = pick(rows, 256)
    scale = math.log2(math.e) / math.sqrt(HEAD_DIM)
    count = len(parts)

    def kernel(which_ref, *refs):
        norm_refs = refs[count : count + 3]
        x_refs, refs = refs[:count], refs[3:]
        w_refs = refs[count : count + kinds]
        acc_refs = refs[count + kinds : count + 2 * kinds]
        gain_ref, col_ref, row_ref, out_ref, held = refs[count + 2 * kinds :]
        step = pl.program_id(0)

        @pl.when(step == 0)
        def _():
            for c in range(kinds):
                held[c] = acc_refs[c][...]

        x = normalize(x_refs, *norm_refs)
        for c in range(kinds):
            held[c] += jnp.dot(x, w_refs[c][...], preferred_element_type=jnp.float32)

        def one_head(h, carry):
            at = pl.ds(pl.multiple_of(h * HEAD_DIM, HEAD_DIM), HEAD_DIM)
            gain = gain_ref[h]
            query = head_norm(held[0, :, at], gain[0:1, :])
            key = head_norm(held[1, :, at], gain[1:2, :])
            value = held[2, :, at].astype(jnp.bfloat16)
            for begin in range(0, rows, tile):
                low = max(0, (begin - reach) // 128 * 128)
                high = min(rows, -(-(begin + tile + reach) // 128) * 128)
                scores = lax.dot_general(
                    query[begin : begin + tile],
                    key[low:high],
                    (((1,), (1,)), ((), ())),
                    preferred_element_type=jnp.float32,
                )
                same = col_ref[begin : begin + tile, :] == row_ref[:, low:high]
                scores = jnp.where(same, scores, NEG)
                top = jnp.max(scores, axis=-1, keepdims=True)
                expo = jnp.exp2((scores - top) * scale)
                total = jnp.sum(expo, axis=-1, keepdims=True)
                weights = (expo * (1.0 / total)).astype(jnp.bfloat16)
                context = jnp.dot(weights, value[low:high], preferred_element_type=jnp.float32)
                out_ref[begin : begin + tile, at] = context.astype(jnp.bfloat16)
            return carry

        @pl.when(step == steps - 1)
        def _():
            lax.fori_loop(0, heads, one_head, 0)

    def w_spec(c):
        return pl.BlockSpec(
            (None, deep, cols), lambda s, w: (c, w[0] * steps + s, first // heads)
        )

    def acc_spec(c):
        return pl.BlockSpec((None, rows, cols), lambda s, w: (c, 0, first // heads))

    in_specs = [pl.BlockSpec((rows, deep), lambda s, w: (0, s)) for _ in parts]
    in_specs += [pl.BlockSpec((rows, 1), lambda s, w: (0, 0))] * 2
    in_specs.append(pl.BlockSpec((1, deep), lambda s, w: (0, w[0] * steps + s)))
    in_specs += [w_spec(c) for c in range(kinds)] + [acc_spec(c) for c in range(kinds)]
    in_specs += [
        pl.BlockSpec((heads, 2, HEAD_DIM), lambda s, w: (first // heads, 0, 0)),
        pl.BlockSpec((rows, 1), lambda s, w: (0, 0)),
        pl.BlockSpec((1, rows), lambda s, w: (0, 0)),
    ]
    return pl.pallas_call(
        kernel,
        grid_spec=pltpu.PrefetchScalarGridSpec(
            num_scalar_prefetch=1,
            grid=(steps,),
            in_specs=in_specs,
            out_specs=pl.BlockSpec((rows, cols), lambda s, w: (0, 0)),
            scratch_shapes=[pltpu.VMEM((kinds, rows, cols), jnp.float32)],
        ),
        out_shape=jax.ShapeDtypeStruct((rows, cols), jnp.bfloat16),
        compiler_params=pltpu.CompilerParams(vmem_limit_bytes=VMEM),
        cost_estimate=COST,
    )(
        jnp.reshape(which, (1,)), *parts, *norm, *([weight] * kinds), *([acc] * kinds),
        gains, block_col, block_row,
    )


def project_out(pieces, weight, which, acc, residual):
    rows = pieces[0][0].shape[0]
    _, depth, _ = weight.shape
    width = which[1]
    high = pick(rows, 256)
    flat = [array for piece in pieces for array in piece]

    def kernel(which_ref, *refs):
        out_ref = refs[-1]
        w_ref = refs[len(flat)]
        total = None if acc is None else refs[len(flat) + 1][...]
        first = begin = 0
        for piece in pieces:
            x = whole(refs[first : first + len(piece)])
            first += len(piece)
            part = jnp.dot(
                x, w_ref[begin : begin + x.shape[1], :], preferred_element_type=jnp.float32
            )
            begin += x.shape[1]
            total = part if total is None else total + part
        if residual is not None:
            total = refs[-2][...].astype(jnp.float32) + total
        out_ref[...] = total.astype(out_ref.dtype)

    tile = pl.BlockSpec((high, width), lambda i, w: (i, 0))
    in_specs = [pl.BlockSpec((high, p.shape[1]), lambda i, w: (i, 0)) for p in flat]
    in_specs.append(pl.BlockSpec((None, depth, width), lambda i, w: (w[0], 0, w[1])))
    args = [jnp.stack([which[0], which[2]]), *flat, weight]
    for extra in (acc, residual):
        if extra is not None:
            in_specs.append(tile)
            args.append(extra)
    out_type = jnp.float32 if residual is None else jnp.bfloat16
    return pl.pallas_call(
        kernel,
        grid_spec=pltpu.PrefetchScalarGridSpec(
            num_scalar_prefetch=1, grid=(rows // high,), in_specs=in_specs, out_specs=tile
        ),
        out_shape=jax.ShapeDtypeStruct((rows, width), out_type),
        compiler_params=pltpu.CompilerParams(vmem_limit_bytes=VMEM),
        cost_estimate=COST,
    )(*args)


def exchange_out_weight(out_weight, n, groups):
    depth, features = out_weight.shape
    place = lax.axis_index("mp")
    piece = depth // groups
    cols = features // n
    mine = lax.dynamic_slice_in_dim(out_weight, lax.axis_index("dp") * piece, piece, axis=0)

    def columns(index):
        return lax.dynamic_slice_in_dim(mine, index * cols, cols, axis=1)

    received = [(place, columns(place))]
    for d in range(1, n):
        sent = lax.ppermute(
            columns((place + d) % n), "mp", [(i, (i + d) % n) for i in range(n)]
        )
        received.append(((place - d) % n, sent))
    return received


def stack(received):
    pieces = jnp.zeros((len(received), *received[0][1].shape), received[0][1].dtype)
    for origin, array in received:
        pieces = lax.dynamic_update_slice_in_dim(pieces, array[None], origin, axis=0)
    return pieces


def shards(tokens, dest_pos, src_row, segment_ids, norm_gain, qkv_weight, qk_gain, out_weight):
    groups = lax.axis_size("dp")
    n = lax.axis_size("mp")
    place = lax.axis_index("mp")
    rows, cols = tokens.shape
    features = cols * n
    reach = 3 * rows // (2 * groups)
    heads = qkv_weight.shape[2] // HEAD_DIM

    segment = lax.all_gather(segment_ids, "dp", tiled=True)[dest_pos]
    block = dest_pos // rows * groups + segment
    block_col = block[:, None]
    block_row = block[None, :]
    gains = jnp.transpose(qk_gain, (1, 0, 2))

    with jax.named_scope("moments"):
        values = tokens.astype(jnp.float32)
        moments = jnp.stack([jnp.sum(values, axis=1), jnp.sum(values * values, axis=1)])
        sums = moments
        for d in range(1, n):
            sums = sums + lax.ppermute(moments, "mp", [(i, (i + d) % n) for i in range(n)])
        average = sums[0] / features
        variance = sums[1] / features - average * average
        inverse = lax.rsqrt(variance + EPS)
        norm = (average[:, None], inverse[:, None], norm_gain[None, :])

    sources = origins("mp", n)

    def step_project(parts, origin, acc):
        with jax.named_scope("project"):
            return project(parts, norm, qkv_weight, origin, acc)

    line = Relay(tokens, "mp", n)
    line.step(1, sums)
    projected = step_project([tokens], place, None)
    pieces = out_weight
    for s in range(2, n):
        there = [line.got[key] for key in line.steps if key[0] == s - 1]
        pieces = line.step(s, projected, block, pieces, *there)[2]
        if s == 2:
            pieces = stack(exchange_out_weight(pieces, n, groups))
        elif s == 3:
            out_columns = lax.all_gather(pieces, "dp", axis=1, tiled=True)
        projected = step_project(line.arrived(s - 2), sources[s - 2], projected)
    last = line.arrived(n - 2)

    chunk = 2 if heads % 2 == 0 else 1
    contexts, lines = [], []
    for first in range(0, heads, chunk):
        if contexts:
            before = [contexts[-1]]
            if len(lines) >= 2:
                before += [lines[-2].got[(1, kind)] for kind in "EO"]
            gains = lax.optimization_barrier((gains, *before))[0]
        with jax.named_scope("attend"):
            context = attend(
                last, norm, qkv_weight, sources[n - 2], projected, gains, block_col, block_row,
                first, chunk, reach,
            )
        contexts.append(context)
        lines.append(Relay(context, "mp", n))
        lines[-1].step(1)

    zero = jnp.zeros((), jnp.int32)

    def step_out(k, acc, residual):
        pieces = [line.arrived(k) for line in lines]
        return project_out(pieces, out_columns, (sources[k], cols, zero), acc, residual)

    lines[0].step(2)
    there = [lines[0].got[key] for key in lines[0].steps if key[0] == 2]
    tied = lax.optimization_barrier((*contexts, *there))[: len(contexts)]
    total = project_out([[c] for c in tied], out_weight[None], (zero, cols, place), None, None)
    for s in range(2, n):
        for line in lines:
            if line is lines[-1]:
                line.step(s, total)
            elif s > 2 or line is not lines[0]:
                line.step(s)
        total = step_out(s - 2, total, None)
    return step_out(n - 2, total, tokens)


def solution(mesh):
    in_specs = (
        P("dp", "mp"),
        P("dp"),
        P("dp"),
        P("dp"),
        P(),
        P(None, None, "mp"),
        P(None, "mp", None),
        P("mp", None),
    )
    out_specs = P("dp", "mp")
    return jax.shard_map(shards, mesh=mesh, in_specs=in_specs, out_specs=out_specs, check_vma=False)
```

```python
import functools
import math

import jax
import jax.numpy as jnp
import numpy as np
from jax import lax
from jax.experimental import pallas as pl
from jax.experimental.pallas import tpu as pltpu
from jax.sharding import PartitionSpec as P

HEAD_DIM = 128
EPS = 1e-06
NEG = -1e30
VMEM = 56 * 1024 * 1024
COST = pl.CostEstimate(flops=15 * 10**9, bytes_accessed=2**20, transcendentals=0)


def pick(total, wanted):
    return max(w for w in range(128, min(total, wanted) + 1, 128) if total % w == 0)


def line_schedule(n):
    steps = {}
    for s in range(1, n):
        for kind, low in (("E", 0), ("O", 1)):
            pairs = []
            for i in range(low, n - 1, 2):
                if i - s + 1 >= 0:
                    pairs.append((i, i + 1))
                if i + s <= n - 1:
                    pairs.append((i + 1, i))
            if pairs:
                steps[(s, kind)] = pairs
    slots = [[] for _ in range(n)]
    for (s, kind), pairs in sorted(steps.items()):
        for source, target in pairs:
            origin = target - s if source < target else target + s
            slots[target].append(((s, kind), origin))
    return steps, slots


class Relay:
    def __init__(self, block, axis, n):
        self.axis, self.n = axis, n
        self.steps, self.slots = line_schedule(n)
        self.got = {(0, "E"): block, (0, "O"): block}

    def step(self, s, *after):
        kinds = [kind for kind in "EO" if (s, kind) in self.steps]
        sources = [self.got[(s - 1, "O" if kind == "E" else "E")] for kind in kinds]
        tied = lax.optimization_barrier((*sources, *after))
        for kind, source in zip(kinds, tied):
            self.got[(s, kind)] = lax.ppermute(source, self.axis, self.steps[(s, kind)])
        return tied[len(kinds) : len(kinds) + len(after)]

    def arrived(self, k):
        keys = sorted({slot[k][0] for slot in self.slots})
        if all({key for key, _ in slot} & set(keys) == {slot[k][0]} for slot in self.slots):
            return [self.got[key] for key in keys]
        place = lax.axis_index(self.axis)
        value = self.got[keys[0]]
        for key in keys[1:]:
            here = np.array([slot[k][0] == key for slot in self.slots])
            value = jnp.where(jnp.asarray(here)[place], self.got[key], value)
        return [value]


def origins(axis, n):
    _, slots = line_schedule(n)
    table = np.array([[slots[i][k][1] for k in range(n - 1)] for i in range(n)], np.int32)
    place = lax.axis_index(axis)
    return [jnp.asarray(table)[place, k] for k in range(n - 1)]


def whole(refs):
    value = refs[0][...]
    for ref in refs[1:]:
        value = value + ref[...]
    return value


def normalize(refs, average_ref, inverse_ref, gain_ref):
    centred = whole(refs).astype(jnp.float32) - average_ref[...]
    return (centred * inverse_ref[...] * gain_ref[...]).astype(jnp.bfloat16)


def project(parts, norm, weight, which, acc):
    rows, depth = parts[0].shape
    kinds, _, width = weight.shape
    cols = pick(width, 768)
    count = len(parts)

    def kernel(which_ref, *refs):
        normed, out_ref = refs[-1], refs[-2]

        @pl.when((pl.program_id(0) == 0) & (pl.program_id(1) == 0))
        def _():
            normed[...] = normalize(refs[:count], *refs[count : count + 3])

        part = jnp.dot(normed[...], refs[count + 3][...], preferred_element_type=jnp.float32)
        if acc is not None:
            part = part + refs[count + 4][...]
        out_ref[...] = part

    tile = pl.BlockSpec((None, rows, cols), lambda c, j, w: (c, 0, j))
    in_specs = [pl.BlockSpec((rows, depth), lambda c, j, w: (0, 0)) for _ in parts]
    in_specs += [pl.BlockSpec((rows, 1), lambda c, j, w: (0, 0))] * 2
    in_specs.append(pl.BlockSpec((1, depth), lambda c, j, w: (0, w[0])))
    in_specs.append(pl.BlockSpec((None, depth, cols), lambda c, j, w: (c, w[0], j)))
    args = [jnp.reshape(which, (1,)), *parts, *norm, weight]
    aliases = {}
    if acc is not None:
        in_specs.append(tile)
        args.append(acc)
        aliases = {len(args) - 1: 0}
    return pl.pallas_call(
        kernel,
        grid_spec=pltpu.PrefetchScalarGridSpec(
            num_scalar_prefetch=1,
            grid=(kinds, width // cols),
            in_specs=in_specs,
            out_specs=tile,
            scratch_shapes=[pltpu.VMEM((rows, depth), jnp.bfloat16)],
        ),
        out_shape=jax.ShapeDtypeStruct((kinds, rows, width), jnp.float32),
        input_output_aliases=aliases,
        compiler_params=pltpu.CompilerParams(vmem_limit_bytes=VMEM),
        cost_estimate=pl.CostEstimate(
            flops=2 * kinds * rows * depth * width,
            bytes_accessed=2 * kinds * depth * width + 8 * kinds * rows * width,
            transcendentals=0,
        ),
    )(*args)


def head_norm(values, gain):
    average = jnp.mean(values, axis=-1, keepdims=True)
    centred = values - average
    variance = jnp.mean(centred * centred, axis=-1, keepdims=True)
    return (centred * lax.rsqrt(variance + EPS) * gain).astype(jnp.bfloat16)


def attend(parts, norm, weight, which, acc, gains, block_col, block_row, first, heads, reach):
    rows, depth = parts[0].shape
    kinds = weight.shape[0]
    cols = heads * HEAD_DIM
    deep = pick(depth, 512)
    steps = depth // deep
    tile = pick(rows, 256)
    scale = math.log2(math.e) / math.sqrt(HEAD_DIM)
    count = len(parts)

    def kernel(which_ref, *refs):
        norm_refs = refs[count : count + 3]
        x_refs, refs = refs[:count], refs[3:]
        w_refs = refs[count : count + kinds]
        acc_refs = refs[count + kinds : count + 2 * kinds]
        gain_ref, col_ref, row_ref, out_ref, held = refs[count + 2 * kinds :]
        step = pl.program_id(0)

        @pl.when(step == 0)
        def _():
            for c in range(kinds):
                held[c] = acc_refs[c][...]

        x = normalize(x_refs, *norm_refs)
        for c in range(kinds):
            held[c] += jnp.dot(x, w_refs[c][...], preferred_element_type=jnp.float32)

        def one_head(h, carry):
            at = pl.ds(pl.multiple_of(h * HEAD_DIM, HEAD_DIM), HEAD_DIM)
            gain = gain_ref[h]
            query = head_norm(held[0, :, at], gain[0:1, :])
            key = head_norm(held[1, :, at], gain[1:2, :])
            value = held[2, :, at].astype(jnp.bfloat16)
            for begin in range(0, rows, tile):
                low = max(0, (begin - reach) // 128 * 128)
                high = min(rows, -(-(begin + tile + reach) // 128) * 128)
                scores = lax.dot_general(
                    query[begin : begin + tile],
                    key[low:high],
                    (((1,), (1,)), ((), ())),
                    preferred_element_type=jnp.float32,
                )
                same = col_ref[begin : begin + tile, :] == row_ref[:, low:high]
                scores = jnp.where(same, scores, NEG)
                top = jnp.max(scores, axis=-1, keepdims=True)
                expo = jnp.exp2((scores - top) * scale)
                total = jnp.sum(expo, axis=-1, keepdims=True)
                weights = (expo * (1.0 / total)).astype(jnp.bfloat16)
                context = jnp.dot(weights, value[low:high], preferred_element_type=jnp.float32)
                out_ref[begin : begin + tile, at] = context.astype(jnp.bfloat16)
            return carry

        @pl.when(step == steps - 1)
        def _():
            lax.fori_loop(0, heads, one_head, 0)

    def w_spec(c):
        return pl.BlockSpec(
            (None, deep, cols), lambda s, w: (c, w[0] * steps + s, first // heads)
        )

    def acc_spec(c):
        return pl.BlockSpec((None, rows, cols), lambda s, w: (c, 0, first // heads))

    in_specs = [pl.BlockSpec((rows, deep), lambda s, w: (0, s)) for _ in parts]
    in_specs += [pl.BlockSpec((rows, 1), lambda s, w: (0, 0))] * 2
    in_specs.append(pl.BlockSpec((1, deep), lambda s, w: (0, w[0] * steps + s)))
    in_specs += [w_spec(c) for c in range(kinds)] + [acc_spec(c) for c in range(kinds)]
    in_specs += [
        pl.BlockSpec((heads, 2, HEAD_DIM), lambda s, w: (first // heads, 0, 0)),
        pl.BlockSpec((rows, 1), lambda s, w: (0, 0)),
        pl.BlockSpec((1, rows), lambda s, w: (0, 0)),
    ]
    return pl.pallas_call(
        kernel,
        grid_spec=pltpu.PrefetchScalarGridSpec(
            num_scalar_prefetch=1,
            grid=(steps,),
            in_specs=in_specs,
            out_specs=pl.BlockSpec((rows, cols), lambda s, w: (0, 0)),
            scratch_shapes=[pltpu.VMEM((kinds, rows, cols), jnp.float32)],
        ),
        out_shape=jax.ShapeDtypeStruct((rows, cols), jnp.bfloat16),
        compiler_params=pltpu.CompilerParams(vmem_limit_bytes=VMEM),
        cost_estimate=COST,
    )(
        jnp.reshape(which, (1,)), *parts, *norm, *([weight] * kinds), *([acc] * kinds),
        gains, block_col, block_row,
    )


def project_out(pieces, weight, which, acc, residual):
    rows = pieces[0][0].shape[0]
    _, depth, _ = weight.shape
    width = which[1]
    high = pick(rows, 512)
    flat = [array for piece in pieces for array in piece]

    def kernel(which_ref, *refs):
        out_ref = refs[-1]
        w_ref = refs[len(flat)]
        total = None if acc is None else refs[len(flat) + 1][...]
        first = begin = 0
        for piece in pieces:
            x = whole(refs[first : first + len(piece)])
            first += len(piece)
            part = jnp.dot(
                x, w_ref[begin : begin + x.shape[1], :], preferred_element_type=jnp.float32
            )
            begin += x.shape[1]
            total = part if total is None else total + part
        if residual is not None:
            total = refs[-2][...].astype(jnp.float32) + total
        out_ref[...] = total.astype(out_ref.dtype)

    tile = pl.BlockSpec((high, width), lambda i, w: (i, 0))
    in_specs = [pl.BlockSpec((high, p.shape[1]), lambda i, w: (i, 0)) for p in flat]
    in_specs.append(pl.BlockSpec((None, depth, width), lambda i, w: (w[0], 0, w[1])))
    args = [jnp.stack([which[0], which[2]]), *flat, weight]
    for extra in (acc, residual):
        if extra is not None:
            in_specs.append(tile)
            args.append(extra)
    out_type = jnp.float32 if residual is None else jnp.bfloat16
    return pl.pallas_call(
        kernel,
        grid_spec=pltpu.PrefetchScalarGridSpec(
            num_scalar_prefetch=1, grid=(rows // high,), in_specs=in_specs, out_specs=tile
        ),
        out_shape=jax.ShapeDtypeStruct((rows, width), out_type),
        compiler_params=pltpu.CompilerParams(vmem_limit_bytes=VMEM),
        cost_estimate=COST,
    )(*args)


def exchange_out_weight(out_weight, n, groups):
    depth, features = out_weight.shape
    place = lax.axis_index("mp")
    piece = depth // groups
    cols = features // n
    mine = lax.dynamic_slice_in_dim(out_weight, lax.axis_index("dp") * piece, piece, axis=0)

    def columns(index):
        return lax.dynamic_slice_in_dim(mine, index * cols, cols, axis=1)

    received = [(place, columns(place))]
    for d in range(1, n):
        sent = lax.ppermute(
            columns((place + d) % n), "mp", [(i, (i + d) % n) for i in range(n)]
        )
        received.append(((place - d) % n, sent))
    return received


def stack(received):
    pieces = jnp.zeros((len(received), *received[0][1].shape), received[0][1].dtype)
    for origin, array in received:
        pieces = lax.dynamic_update_slice_in_dim(pieces, array[None], origin, axis=0)
    return pieces


def shards(tokens, dest_pos, src_row, segment_ids, norm_gain, qkv_weight, qk_gain, out_weight):
    groups = lax.axis_size("dp")
    n = lax.axis_size("mp")
    place = lax.axis_index("mp")
    rows, cols = tokens.shape
    features = cols * n
    reach = 3 * rows // (2 * groups)
    heads = qkv_weight.shape[2] // HEAD_DIM

    segment = lax.all_gather(segment_ids, "dp", tiled=True)[dest_pos]
    block = dest_pos // rows * groups + segment
    block_col = block[:, None]
    block_row = block[None, :]
    gains = jnp.transpose(qk_gain, (1, 0, 2))

    with jax.named_scope("moments"):
        values = tokens.astype(jnp.float32)
        moments = jnp.stack([jnp.sum(values, axis=1), jnp.sum(values * values, axis=1)])
        sums = moments
        for d in range(1, n):
            sums = sums + lax.ppermute(moments, "mp", [(i, (i + d) % n) for i in range(n)])

    sources = origins("mp", n)

    def step_project(parts, origin, acc):
        with jax.named_scope("project"):
            return project(parts, norm, qkv_weight, origin, acc)

    line = Relay(tokens, "mp", n)
    line.step(1)
    projected = None
    for s in range(2, n):
        there = [line.got[key] for key in line.steps if key[0] == s - 1]
        ready = [] if projected is None else [projected]
        _, sums, *ready = line.step(s, block, sums, *ready, *there)[: 2 + len(ready)]
        if s == 2:
            average = sums[0] / features
            variance = sums[1] / features - average * average
            inverse = lax.rsqrt(variance + EPS)
            norm = (average[:, None], inverse[:, None], norm_gain[None, :])
            projected = step_project([tokens], place, None)
            pieces = lax.optimization_barrier((out_weight, projected))[0]
            received = exchange_out_weight(pieces, n, groups)
        else:
            projected = ready[0]
        projected = step_project(line.arrived(s - 2), sources[s - 2], projected)
    last = line.arrived(n - 2)

    chunk = 2 if heads % 2 == 0 else 1
    contexts, lines = [], []
    for first in range(0, heads, chunk):
        if contexts:
            before = [contexts[-1]]
            if len(lines) >= 2:
                before += [lines[-2].got[(1, kind)] for kind in "EO"]
            gains = lax.optimization_barrier((gains, *before))[0]
        with jax.named_scope("attend"):
            context = attend(
                last, norm, qkv_weight, sources[n - 2], projected, gains, block_col, block_row,
                first, chunk, reach,
            )
        contexts.append(context)
        lines.append(Relay(context, "mp", n))
        lines[-1].step(1)

    pieces = lax.optimization_barrier((*[array for _, array in received], contexts[0]))
    pieces = stack([(origin, array) for (origin, _), array in zip(received, pieces)])
    out_columns = lax.all_gather(pieces, "dp", axis=1, tiled=True)
    zero = jnp.zeros((), jnp.int32)

    def step_out(k, acc, residual):
        pieces = [line.arrived(k) for line in lines]
        return project_out(pieces, out_columns, (sources[k], cols, zero), acc, residual)

    lines[0].step(2)
    there = [lines[0].got[key] for key in lines[0].steps if key[0] == 2]
    tied = lax.optimization_barrier((*contexts, *there))[: len(contexts)]
    total = project_out([[c] for c in tied], out_weight[None], (zero, cols, place), None, None)
    for s in range(2, n):
        for line in lines:
            if line is lines[-1]:
                line.step(s, total)
            elif s > 2 or line is not lines[0]:
                line.step(s)
        total = step_out(s - 2, total, None)
    return step_out(n - 2, total, tokens)


def solution(mesh):
    in_specs = (
        P("dp", "mp"),
        P("dp"),
        P("dp"),
        P("dp"),
        P(),
        P(None, None, "mp"),
        P(None, "mp", None),
        P("mp", None),
    )
    out_specs = P("dp", "mp")
    return jax.shard_map(shards, mesh=mesh, in_specs=in_specs, out_specs=out_specs, check_vma=False)
```

```python
import functools
import math

import jax
import jax.numpy as jnp
import numpy as np
from jax import lax
from jax.experimental import pallas as pl
from jax.experimental.pallas import tpu as pltpu
from jax.sharding import PartitionSpec as P

HEAD_DIM = 128
EPS = 1e-06
NEG = -1e30
VMEM = 56 * 1024 * 1024
COST = pl.CostEstimate(flops=15 * 10**9, bytes_accessed=2**20, transcendentals=0)


def pick(total, wanted):
    return max(w for w in range(128, min(total, wanted) + 1, 128) if total % w == 0)


def line_schedule(n):
    steps = {}
    for s in range(1, n):
        for kind, low in (("E", 0), ("O", 1)):
            pairs = []
            for i in range(low, n - 1, 2):
                if i - s + 1 >= 0:
                    pairs.append((i, i + 1))
                if i + s <= n - 1:
                    pairs.append((i + 1, i))
            if pairs:
                steps[(s, kind)] = pairs
    slots = [[] for _ in range(n)]
    for (s, kind), pairs in sorted(steps.items()):
        for source, target in pairs:
            origin = target - s if source < target else target + s
            slots[target].append(((s, kind), origin))
    return steps, slots


class Relay:
    def __init__(self, block, axis, n):
        self.axis, self.n = axis, n
        self.steps, self.slots = line_schedule(n)
        self.got = {(0, "E"): block, (0, "O"): block}

    def step(self, s, *after):
        kinds = [kind for kind in "EO" if (s, kind) in self.steps]
        sources = [self.got[(s - 1, "O" if kind == "E" else "E")] for kind in kinds]
        tied = lax.optimization_barrier((*sources, *after))
        for kind, source in zip(kinds, tied):
            self.got[(s, kind)] = lax.ppermute(source, self.axis, self.steps[(s, kind)])
        return tied[len(kinds) : len(kinds) + len(after)]

    def arrived(self, k):
        keys = sorted({slot[k][0] for slot in self.slots})
        if all({key for key, _ in slot} & set(keys) == {slot[k][0]} for slot in self.slots):
            return [self.got[key] for key in keys]
        place = lax.axis_index(self.axis)
        value = self.got[keys[0]]
        for key in keys[1:]:
            here = np.array([slot[k][0] == key for slot in self.slots])
            value = jnp.where(jnp.asarray(here)[place], self.got[key], value)
        return [value]


def origins(axis, n):
    _, slots = line_schedule(n)
    table = np.array([[slots[i][k][1] for k in range(n - 1)] for i in range(n)], np.int32)
    place = lax.axis_index(axis)
    return [jnp.asarray(table)[place, k] for k in range(n - 1)]


def whole(refs):
    value = refs[0][...]
    for ref in refs[1:]:
        value = value + ref[...]
    return value


def normalize(refs, average_ref, inverse_ref, gain_ref):
    centred = whole(refs).astype(jnp.float32) - average_ref[...]
    return (centred * inverse_ref[...] * gain_ref[...]).astype(jnp.bfloat16)


def project(parts, norm, weight, which, acc):
    rows, depth = parts[0].shape
    kinds, _, width = weight.shape
    cols = pick(width, 768)
    count = len(parts)

    def kernel(which_ref, *refs):
        normed, out_ref = refs[-1], refs[-2]

        @pl.when((pl.program_id(0) == 0) & (pl.program_id(1) == 0))
        def _():
            normed[...] = normalize(refs[:count], *refs[count : count + 3])

        part = jnp.dot(normed[...], refs[count + 3][...], preferred_element_type=jnp.float32)
        if acc is not None:
            part = part + refs[count + 4][...]
        out_ref[...] = part

    tile = pl.BlockSpec((None, rows, cols), lambda c, j, w: (c, 0, j))
    in_specs = [pl.BlockSpec((rows, depth), lambda c, j, w: (0, 0)) for _ in parts]
    in_specs += [pl.BlockSpec((rows, 1), lambda c, j, w: (0, 0))] * 2
    in_specs.append(pl.BlockSpec((1, depth), lambda c, j, w: (0, w[0])))
    in_specs.append(pl.BlockSpec((None, depth, cols), lambda c, j, w: (c, w[0], j)))
    args = [jnp.reshape(which, (1,)), *parts, *norm, weight]
    aliases = {}
    if acc is not None:
        in_specs.append(tile)
        args.append(acc)
        aliases = {len(args) - 1: 0}
    return pl.pallas_call(
        kernel,
        grid_spec=pltpu.PrefetchScalarGridSpec(
            num_scalar_prefetch=1,
            grid=(kinds, width // cols),
            in_specs=in_specs,
            out_specs=tile,
            scratch_shapes=[pltpu.VMEM((rows, depth), jnp.bfloat16)],
        ),
        out_shape=jax.ShapeDtypeStruct((kinds, rows, width), jnp.float32),
        input_output_aliases=aliases,
        compiler_params=pltpu.CompilerParams(vmem_limit_bytes=VMEM),
        cost_estimate=pl.CostEstimate(
            flops=2 * kinds * rows * depth * width,
            bytes_accessed=2 * kinds * depth * width + 8 * kinds * rows * width,
            transcendentals=0,
        ),
    )(*args)


def head_norm(values, gain):
    average = jnp.mean(values, axis=-1, keepdims=True)
    centred = values - average
    variance = jnp.mean(centred * centred, axis=-1, keepdims=True)
    return (centred * lax.rsqrt(variance + EPS) * gain).astype(jnp.bfloat16)


def attend(parts, norm, weight, which, acc, gains, block_col, block_row, first, heads, reach):
    rows, depth = parts[0].shape
    kinds = weight.shape[0]
    cols = heads * HEAD_DIM
    deep = pick(depth, 768)
    steps = depth // deep
    tile = pick(rows, 512)
    scale = math.log2(math.e) / math.sqrt(HEAD_DIM)
    count = len(parts)

    def kernel(which_ref, *refs):
        norm_refs = refs[count : count + 3]
        x_refs, refs = refs[:count], refs[3:]
        w_refs = refs[count : count + kinds]
        acc_refs = refs[count + kinds : count + 2 * kinds]
        gain_ref, col_ref, row_ref, out_ref, held = refs[count + 2 * kinds :]
        step = pl.program_id(0)

        @pl.when(step == 0)
        def _():
            for c in range(kinds):
                held[c] = acc_refs[c][...]

        x = normalize(x_refs, *norm_refs)
        for c in range(kinds):
            held[c] += jnp.dot(x, w_refs[c][...], preferred_element_type=jnp.float32)

        def one_head(h, carry):
            at = pl.ds(pl.multiple_of(h * HEAD_DIM, HEAD_DIM), HEAD_DIM)
            gain = gain_ref[h]
            query = head_norm(held[0, :, at], gain[0:1, :])
            key = head_norm(held[1, :, at], gain[1:2, :])
            value = held[2, :, at].astype(jnp.bfloat16)
            for begin in range(0, rows, tile):
                low = max(0, (begin - reach) // 128 * 128)
                high = min(rows, -(-(begin + tile + reach) // 128) * 128)
                scores = lax.dot_general(
                    query[begin : begin + tile],
                    key[low:high],
                    (((1,), (1,)), ((), ())),
                    preferred_element_type=jnp.float32,
                )
                same = col_ref[begin : begin + tile, :] == row_ref[:, low:high]
                scores = jnp.where(same, scores, NEG)
                top = jnp.max(scores, axis=-1, keepdims=True)
                expo = jnp.exp2((scores - top) * scale)
                total = jnp.sum(expo, axis=-1, keepdims=True)
                weights = (expo * (1.0 / total)).astype(jnp.bfloat16)
                context = jnp.dot(weights, value[low:high], preferred_element_type=jnp.float32)
                out_ref[begin : begin + tile, at] = context.astype(jnp.bfloat16)
            return carry

        @pl.when(step == steps - 1)
        def _():
            lax.fori_loop(0, heads, one_head, 0)

    def w_spec(c):
        return pl.BlockSpec(
            (None, deep, cols), lambda s, w: (c, w[0] * steps + s, first // heads)
        )

    def acc_spec(c):
        return pl.BlockSpec((None, rows, cols), lambda s, w: (c, 0, first // heads))

    in_specs = [pl.BlockSpec((rows, deep), lambda s, w: (0, s)) for _ in parts]
    in_specs += [pl.BlockSpec((rows, 1), lambda s, w: (0, 0))] * 2
    in_specs.append(pl.BlockSpec((1, deep), lambda s, w: (0, w[0] * steps + s)))
    in_specs += [w_spec(c) for c in range(kinds)] + [acc_spec(c) for c in range(kinds)]
    in_specs += [
        pl.BlockSpec((heads, 2, HEAD_DIM), lambda s, w: (first // heads, 0, 0)),
        pl.BlockSpec((rows, 1), lambda s, w: (0, 0)),
        pl.BlockSpec((1, rows), lambda s, w: (0, 0)),
    ]
    return pl.pallas_call(
        kernel,
        grid_spec=pltpu.PrefetchScalarGridSpec(
            num_scalar_prefetch=1,
            grid=(steps,),
            in_specs=in_specs,
            out_specs=pl.BlockSpec((rows, cols), lambda s, w: (0, 0)),
            scratch_shapes=[pltpu.VMEM((kinds, rows, cols), jnp.float32)],
        ),
        out_shape=jax.ShapeDtypeStruct((rows, cols), jnp.bfloat16),
        compiler_params=pltpu.CompilerParams(vmem_limit_bytes=VMEM),
        cost_estimate=COST,
    )(
        jnp.reshape(which, (1,)), *parts, *norm, *([weight] * kinds), *([acc] * kinds),
        gains, block_col, block_row,
    )


def project_out(pieces, weight, which, acc, residual):
    rows = pieces[0][0].shape[0]
    _, depth, _ = weight.shape
    width = which[1]
    high = pick(rows, 512)
    flat = [array for piece in pieces for array in piece]

    def kernel(which_ref, *refs):
        out_ref = refs[-1]
        w_ref = refs[len(flat)]
        total = None if acc is None else refs[len(flat) + 1][...]
        first = begin = 0
        for piece in pieces:
            x = whole(refs[first : first + len(piece)])
            first += len(piece)
            part = jnp.dot(
                x, w_ref[begin : begin + x.shape[1], :], preferred_element_type=jnp.float32
            )
            begin += x.shape[1]
            total = part if total is None else total + part
        if residual is not None:
            total = refs[-2][...].astype(jnp.float32) + total
        out_ref[...] = total.astype(out_ref.dtype)

    tile = pl.BlockSpec((high, width), lambda i, w: (i, 0))
    in_specs = [pl.BlockSpec((high, p.shape[1]), lambda i, w: (i, 0)) for p in flat]
    in_specs.append(pl.BlockSpec((None, depth, width), lambda i, w: (w[0], 0, w[1])))
    args = [jnp.stack([which[0], which[2]]), *flat, weight]
    for extra in (acc, residual):
        if extra is not None:
            in_specs.append(tile)
            args.append(extra)
    out_type = jnp.float32 if residual is None else jnp.bfloat16
    return pl.pallas_call(
        kernel,
        grid_spec=pltpu.PrefetchScalarGridSpec(
            num_scalar_prefetch=1, grid=(rows // high,), in_specs=in_specs, out_specs=tile
        ),
        out_shape=jax.ShapeDtypeStruct((rows, width), out_type),
        compiler_params=pltpu.CompilerParams(vmem_limit_bytes=VMEM),
        cost_estimate=COST,
    )(*args)


def exchange_out_weight(out_weight, n, groups):
    depth, features = out_weight.shape
    place = lax.axis_index("mp")
    piece = depth // groups
    cols = features // n
    mine = lax.dynamic_slice_in_dim(out_weight, lax.axis_index("dp") * piece, piece, axis=0)

    def columns(index):
        return lax.dynamic_slice_in_dim(mine, index * cols, cols, axis=1)

    received = [(place, columns(place))]
    for d in range(1, n):
        sent = lax.ppermute(
            columns((place + d) % n), "mp", [(i, (i + d) % n) for i in range(n)]
        )
        received.append(((place - d) % n, sent))
    return received


def stack(received):
    pieces = jnp.zeros((len(received), *received[0][1].shape), received[0][1].dtype)
    for origin, array in received:
        pieces = lax.dynamic_update_slice_in_dim(pieces, array[None], origin, axis=0)
    return pieces


def shards(tokens, dest_pos, src_row, segment_ids, norm_gain, qkv_weight, qk_gain, out_weight):
    groups = lax.axis_size("dp")
    n = lax.axis_size("mp")
    place = lax.axis_index("mp")
    rows, cols = tokens.shape
    features = cols * n
    reach = 3 * rows // (2 * groups)
    heads = qkv_weight.shape[2] // HEAD_DIM

    segment = lax.all_gather(segment_ids, "dp", tiled=True)[dest_pos]
    block = dest_pos // rows * groups + segment
    block_col = block[:, None]
    block_row = block[None, :]
    gains = jnp.transpose(qk_gain, (1, 0, 2))

    with jax.named_scope("moments"):
        values = tokens.astype(jnp.float32)
        moments = jnp.stack([jnp.sum(values, axis=1), jnp.sum(values * values, axis=1)])
        sums = moments
        for d in range(1, n):
            sums = sums + lax.ppermute(moments, "mp", [(i, (i + d) % n) for i in range(n)])

    sources = origins("mp", n)

    def step_project(parts, origin, acc):
        with jax.named_scope("project"):
            return project(parts, norm, qkv_weight, origin, acc)

    line = Relay(tokens, "mp", n)
    line.step(1)
    projected = None
    for s in range(2, n):
        there = [line.got[key] for key in line.steps if key[0] == s - 1]
        ready = [] if projected is None else [projected]
        _, sums, *ready = line.step(s, block, sums, *ready, *there)[: 2 + len(ready)]
        if s == 2:
            average = sums[0] / features
            variance = sums[1] / features - average * average
            inverse = lax.rsqrt(variance + EPS)
            norm = (average[:, None], inverse[:, None], norm_gain[None, :])
            projected = step_project([tokens], place, None)
            pieces = lax.optimization_barrier((out_weight, projected))[0]
            received = exchange_out_weight(pieces, n, groups)
        else:
            projected = ready[0]
        projected = step_project(line.arrived(s - 2), sources[s - 2], projected)
    last = line.arrived(n - 2)

    chunk = 2 if heads % 2 == 0 else 1
    contexts, lines = [], []
    for first in range(0, heads, chunk):
        if contexts:
            before = [contexts[-1]]
            if len(lines) >= 2:
                before += [lines[-2].got[(1, kind)] for kind in "EO"]
            gains = lax.optimization_barrier((gains, *before))[0]
        with jax.named_scope("attend"):
            context = attend(
                last, norm, qkv_weight, sources[n - 2], projected, gains, block_col, block_row,
                first, chunk, reach,
            )
        contexts.append(context)
        lines.append(Relay(context, "mp", n))
        lines[-1].step(1)

    pieces = lax.optimization_barrier((*[array for _, array in received], contexts[0]))
    pieces = stack([(origin, array) for (origin, _), array in zip(received, pieces)])
    out_columns = lax.all_gather(pieces, "dp", axis=1, tiled=True)
    zero = jnp.zeros((), jnp.int32)

    def step_out(k, acc, residual):
        pieces = [line.arrived(k) for line in lines]
        return project_out(pieces, out_columns, (sources[k], cols, zero), acc, residual)

    lines[0].step(2)
    there = [lines[0].got[key] for key in lines[0].steps if key[0] == 2]
    tied = lax.optimization_barrier((*contexts, *there))[: len(contexts)]
    total = project_out([[c] for c in tied], out_weight[None], (zero, cols, place), None, None)
    for s in range(2, n):
        for line in lines:
            if line is lines[-1]:
                line.step(s, total)
            elif s > 2 or line is not lines[0]:
                line.step(s)
        total = step_out(s - 2, total, None)
    return step_out(n - 2, total, tokens)


def solution(mesh):
    in_specs = (
        P("dp", "mp"),
        P("dp"),
        P("dp"),
        P("dp"),
        P(),
        P(None, None, "mp"),
        P(None, "mp", None),
        P("mp", None),
    )
    out_specs = P("dp", "mp")
    return jax.shard_map(shards, mesh=mesh, in_specs=in_specs, out_specs=out_specs, check_vma=False)
```
